1024 devices in a mesh: dp: 16 (over x, y), expert: 64 (over z, core).
Axes of the slice: x: 4, y: 4, z: 32, core: 2. Of those that a mesh axis runs over, the one named last changes fastest.
Arguments:
- tokens: bfloat16 [1024, 196, 768], P(('dp', 'expert')), may hold values from -24 to 24, as said below
- router: bfloat16 [768, 64], replicated, may hold values from -1 to 1, as said below
- w_in: bfloat16 [64, 768, 3072], P('expert', None, 'dp'), may hold values from -0.21875 to 0.21875
- w_out: bfloat16 [64, 3072, 768], P('expert', 'dp'), may hold values from -0.109375 to 0.109375
- out_grad: bfloat16 [1024, 196, 768], P(('dp', 'expert')), may hold values from -6 to 6
Outputs:
- token_grad: bfloat16 [1024, 196, 768], P(('dp', 'expert'))
- router_grad: float32 [768, 64], replicated
- w_in_grad: float32 [64, 768, 3072], P('expert', None, 'dp')
- w_out_grad: float32 [64, 3072, 768], P('expert', 'dp')
The draws below stay inside these ranges and needn't reach their ends.
Inputs may be any that keep to these rules, and one draw needn't show every extreme that they name: Entries of the tokens stay within the bounds. `router`: entries of the slot parameters stay within the bounds.
All inputs are finite; a program needn't handle non-finite values.
Results may differ from the reference program's by a relative error of at most 0.022.
Values may be sent and summed in bfloat16 or wider, within the bound.
No kernel may reach another device: no remote copies, remote signals or barrier semaphores. Data moves between devices by JAX's collectives and lax.ppermute only.
A program may use at most 32 MiB of HBM per device.

```python
import jax
import jax.numpy as jnp
from jax import lax

D = 768
FF = 3072
M = 196
EXPERTS = 64
IMAGES = 1024
N_DP = 16


def draw_router(key, part):
    key = jax.random.fold_in(key, 7)
    values = jnp.clip(jax.random.normal(key, (D, EXPERTS), jnp.float32), -4.0, 4.0) * D ** (-0.5)
    return values.astype(jnp.bfloat16)


def draw_tokens(key, part):
    key = jax.random.fold_in(key, 5)
    keys = jax.random.split(key, 1)
    base = jnp.clip(jax.random.normal(keys[0], (IMAGES, M, D), jnp.float32), -6.0, 6.0)
    return base.astype(jnp.bfloat16)


def shard_levels(key, dims, cuts, least, high):
    loudness = 1.0
    for position, parts in cuts:
        steps = jax.random.uniform(jax.random.fold_in(jax.random.fold_in(key, 6), position), (parts,), jnp.float32, least / len(cuts), high / len(cuts))
        loudness = loudness * jnp.repeat(jnp.exp(steps), dims[position] // parts).reshape((-1,) + (1,) * (len(dims) - 1 - position))
    return loudness


def gaussian(key, dims, scale, bound, cuts=(), kind=jnp.bfloat16):
    loudness = shard_levels(key, dims, cuts, -0.22, 0.18) if cuts else 1.0
    entries = jax.random.normal(key, dims, jnp.float32) * scale * loudness
    return jnp.minimum(jnp.maximum(entries, -bound), bound).astype(kind)


def setup_inputs(seed: int = 0) -> dict:
    splits = jax.random.split(jax.random.key(seed), 6)
    tokens = draw_tokens(jax.random.fold_in(splits[5], 71), 0)
    router = draw_router(jax.random.fold_in(splits[5], 71), 0)
    w_in = gaussian(splits[2], (EXPERTS, D, FF), D ** -0.5, 0.21875, ((0, 64), (2, 16)))
    w_out = gaussian(splits[3], (EXPERTS, FF, D), FF ** -0.5, 0.109375, ((0, 64), (1, 16)))
    out_grad = gaussian(splits[4], (IMAGES, M, D), 1.0, 6.0, ((0, 1024),))
    return {"tokens": tokens, "router": router, "w_in": w_in, "w_out": w_out, "out_grad": out_grad}


def gelu_exact(value):
    return 0.5 * value * (1.0 + jax.scipy.special.erf(value * 0.7071067811865476))


def gelu_slope(value):
    return 0.5 * (1.0 + jax.scipy.special.erf(value * 0.7071067811865476)) + value * jnp.exp(-0.5 * value * value) * 0.3989422804014327


def reference(tokens, router, w_in, w_out, out_grad):
    tok32 = tokens.astype(jnp.float32)
    grad32 = out_grad.astype(jnp.float32)
    rout32 = router.astype(jnp.float32)
    logits = jnp.einsum('bmd,de->bme', tok32, rout32)
    dispatch = jax.nn.softmax(logits, axis=1)
    combine = jax.nn.softmax(logits, axis=2)
    dispatch_b = dispatch.astype(jnp.bfloat16)
    combine_b = combine.astype(jnp.bfloat16)
    slots = jnp.einsum('bme,bmd->ebd', dispatch_b.astype(jnp.float32), tok32).astype(jnp.bfloat16)
    slot_grad = jnp.einsum('bme,bmd->ebd', combine_b.astype(jnp.float32), grad32).astype(jnp.bfloat16)
    blocks = N_DP
    block_width = FF // N_DP

    def per_expert(items):
        rows_in, rows_grad, first, second = items
        count = rows_in.shape[0]
        hidden = jnp.dot(rows_in, first, preferred_element_type=jnp.float32)
        act = gelu_exact(hidden).astype(jnp.bfloat16)
        act_blocks = act.reshape(count, blocks, block_width).astype(jnp.float32)
        second_blocks = second.reshape(blocks, block_width, D).astype(jnp.float32)
        partial_out = jnp.einsum('bkf,kfd->kbd', act_blocks, second_blocks).astype(jnp.bfloat16)
        expert_out = jnp.sum(partial_out.astype(jnp.float32), axis=0).astype(jnp.bfloat16)
        act_grad = jnp.einsum('bd,fd->bf', rows_grad.astype(jnp.float32), second.astype(jnp.float32))
        pre_grad = (act_grad * gelu_slope(hidden)).astype(jnp.bfloat16)
        out_weight_grad = jnp.dot(act.T, rows_grad, preferred_element_type=jnp.float32)
        in_weight_grad = jnp.dot(rows_in.T, pre_grad, preferred_element_type=jnp.float32)
        pre_blocks = pre_grad.reshape(count, blocks, block_width).astype(jnp.float32)
        first_blocks = first.reshape(D, blocks, block_width).astype(jnp.float32)
        partial_in = jnp.einsum('bkf,dkf->kbd', pre_blocks, first_blocks).astype(jnp.bfloat16)
        slot_in = jnp.sum(partial_in.astype(jnp.float32), axis=0).astype(jnp.bfloat16)
        return expert_out, slot_in, in_weight_grad, out_weight_grad

    expert_out, slot_in_grad, w_in_grad, w_out_grad = lax.map(per_expert, (slots, slot_grad, w_in, w_out))
    expert_out = expert_out.astype(jnp.float32)
    slot_in32 = slot_in_grad.astype(jnp.float32)
    combine_dot = jnp.einsum('bmd,ebd->bme', grad32, expert_out)
    combine_part = combine * (combine_dot - jnp.sum(combine * combine_dot, axis=2, keepdims=True))
    dispatch_dot = jnp.einsum('bmd,ebd->bme', tok32, slot_in32)
    dispatch_part = dispatch * (dispatch_dot - jnp.sum(dispatch * dispatch_dot, axis=1, keepdims=True))
    logit_grad = (combine_part + dispatch_part).astype(jnp.bfloat16).astype(jnp.float32)
    token_grad = jnp.einsum('bme,de->bmd', logit_grad, rout32) + jnp.einsum('bme,ebd->bmd', dispatch_b.astype(jnp.float32), slot_in32)
    router_grad = jnp.einsum('bmd,bme->de', tok32, logit_grad)
    return token_grad.astype(jnp.bfloat16), router_grad, w_in_grad, w_out_grad
```

```python
import jax
import jax.numpy as jnp
import numpy as np
from jax import lax
from jax.sharding import Mesh
from jax.sharding import PartitionSpec as P

BF = jnp.bfloat16
F32 = jnp.float32
ALL = ("x", "y", "z", "c")


def gelu_exact(value):
    return 0.5 * value * (1.0 + jax.scipy.special.erf(value * 0.7071067811865476))


def gelu_slope(value):
    return (
        0.5 * (1.0 + jax.scipy.special.erf(value * 0.7071067811865476))
        + value * jnp.exp(-0.5 * value * value) * 0.3989422804014327
    )


def exchange(parts, axes):
    return lax.all_to_all(parts, axes, split_axis=0, concat_axis=0, tiled=True)


def spread(mine, axes, count):
    return exchange(jnp.broadcast_to(mine[None], (count, *mine.shape)), axes)


def dot(a, b, dims):
    return lax.dot_general(a, b, (dims, ((), ())), preferred_element_type=F32)


def sum_of_all(local, nx, ny, nz, nc):
    experts, width = local.shape
    plane = nx * ny * nc
    pieces = local.astype(BF).reshape(plane, experts // plane, width)
    mine = exchange(pieces, ("x", "y", "c")).astype(F32).sum(axis=0).astype(BF)
    total = spread(mine, "z", nz).astype(F32).sum(axis=0).astype(BF)
    return spread(total, ("x", "y", "c"), plane).reshape(experts, width).astype(F32)


def per_device(nx, ny, nz, nc, tokens, router, w_in, w_out, out_grad):
    tok, og = tokens[0], out_grad[0]
    width = tok.shape[1]
    experts = nz * nc
    block = w_in.shape[2]

    weights = jnp.concatenate([w_in[0].T, w_out[0]], axis=0)
    gathered = lax.all_gather(weights, "x", axis=0, tiled=False)
    first = gathered[:, :block].reshape(nx * block, width)
    second = gathered[:, block:].reshape(nx * block, width)

    logits = jnp.dot(tok, router, preferred_element_type=F32)
    dispatch = jax.nn.softmax(logits, axis=0)
    combine = jax.nn.softmax(logits, axis=1)
    dispatch_b = dispatch.astype(BF)
    combine_b = combine.astype(BF)
    slots = dot(dispatch_b, tok, ((0,), (0,))).astype(BF)
    slot_grad = dot(combine_b, og, ((0,), (0,))).astype(BF)
    sent = jnp.stack([slots, slot_grad], axis=1)
    mine = exchange(sent, ("z", "c"))
    pair = jnp.stack([mine[:, 0], mine[:, 1]], axis=0)
    rows = spread(pair, "y", ny)
    rows_in = rows[:, 0].reshape(ny * experts, width)
    rows_grad = rows[:, 1].reshape(ny * experts, width)

    hidden = dot(rows_in, first, ((1,), (1,)))
    act = gelu_exact(hidden).astype(BF)
    act_grad = dot(rows_grad, second, ((1,), (1,)))
    pre_grad = (act_grad * gelu_slope(hidden)).astype(BF)
    partial_out = dot(act, second, ((1,), (0,))).astype(BF)
    partial_in = dot(pre_grad, first, ((1,), (0,))).astype(BF)
    partial = jnp.stack(
        [partial_out.reshape(ny, experts, width), partial_in.reshape(ny, experts, width)], axis=1
    )
    summed = exchange(partial, "y").astype(F32).sum(axis=0).astype(BF)
    back = exchange(jnp.stack([summed[0], summed[1]], axis=1), ("z", "c"))
    expert_out, slot_in_grad = back[:, 0], back[:, 1]

    out_part = dot(act, rows_grad, ((0,), (0,))).reshape(nx, block, width)
    in_part = dot(pre_grad, rows_in, ((0,), (0,))).reshape(nx, block, width)
    parts = jnp.concatenate([in_part, out_part], axis=1)
    grads = lax.psum_scatter(parts.astype(BF), "x", scatter_dimension=0, tiled=False).astype(F32)

    combine_dot = dot(og, expert_out, ((1,), (1,)))
    combine_part = combine * (combine_dot - jnp.sum(combine * combine_dot, axis=1, keepdims=True))
    dispatch_dot = dot(tok, slot_in_grad, ((1,), (1,)))
    dispatch_part = dispatch * (
        dispatch_dot - jnp.sum(dispatch * dispatch_dot, axis=0, keepdims=True)
    )
    logit_grad = (combine_part + dispatch_part).astype(BF)
    router_local = dot(logit_grad, tok, ((0,), (0,)))
    router_grad = sum_of_all(router_local, nx, ny, nz, nc).T
    token_grad = dot(logit_grad, router, ((1,), (1,))) + dot(
        dispatch_b, slot_in_grad, ((1,), (0,))
    )
    return token_grad.astype(BF)[None], router_grad, grads[:block].T[None], grads[block:][None]


def solution(mesh):
    dp, expert = mesh.shape["dp"], mesh.shape["expert"]
    nx, ny, nz, nc = 4, dp // 4, expert // 2, 2
    fine = Mesh(np.asarray(mesh.devices).reshape(nx, ny, nz, nc), ALL)

    def run(*args):
        return per_device(nx, ny, nz, nc, *args)

    return jax.shard_map(
        run,
        mesh=fine,
        in_specs=(
            P(ALL, None, None),
            P(),
            P(("z", "c"), None, ("x", "y")),
            P(("z", "c"), ("x", "y"), None),
            P(ALL, None, None),
        ),
        out_specs=(
            P(ALL, None, None),
            P(),
            P(("z", "c"), None, ("x", "y")),
            P(("z", "c"), ("x", "y"), None),
        ),
        check_vma=False,
    )
```

```python
import jax
import jax.numpy as jnp
import numpy as np
from jax import lax
from jax.experimental import pallas as pl
from jax.experimental.pallas import tpu as pltpu
from jax.sharding import Mesh
from jax.sharding import PartitionSpec as P

BF = jnp.bfloat16
F32 = jnp.float32
ALL = ("x", "y", "z", "c")


def exchange(parts, axes):
    return lax.all_to_all(parts, axes, split_axis=0, concat_axis=0, tiled=True)


def spread(mine, axes, count):
    return exchange(jnp.broadcast_to(mine[None], (count, *mine.shape)), axes)


def dot(a, b, dims):
    return lax.dot_general(a, b, (dims, ((), ())), preferred_element_type=F32)


def expert_kernel(rows_ref, first_ref, second_ref, partial_ref, act_ref, pre_ref, out_sum, in_sum):
    step = pl.program_id(0)
    count, width = out_sum.shape
    rows_in = rows_ref[:, 0].reshape(count, width)
    rows_grad = rows_ref[:, 1].reshape(count, width)
    first, second = first_ref[0], second_ref[0]
    hidden = dot(rows_in, first, ((1,), (1,)))
    act_grad = dot(rows_grad, second, ((1,), (1,)))
    cdf = 0.5 * (1.0 + lax.erf(hidden * 0.7071067811865476))
    slope = cdf + hidden * jnp.exp(-0.5 * hidden * hidden) * 0.3989422804014327
    act = (hidden * cdf).astype(BF)
    pre_grad = (act_grad * slope).astype(BF)
    act_ref[0] = act
    pre_ref[0] = pre_grad
    out_part = dot(act, second, ((1,), (0,)))
    in_part = dot(pre_grad, first, ((1,), (0,)))

    @pl.when(step == 0)
    def _():
        out_sum[...] = out_part
        in_sum[...] = in_part

    @pl.when(step > 0)
    def _():
        out_sum[...] += out_part
        in_sum[...] += in_part

    @pl.when(step == pl.num_programs(0) - 1)
    def _():
        shape = partial_ref.shape[:1] + partial_ref.shape[2:]
        partial_ref[:, 0] = out_sum[...].astype(BF).reshape(shape)
        partial_ref[:, 1] = in_sum[...].astype(BF).reshape(shape)


def expert_parts(rows, first, second):
    ny, _, images, width = rows.shape
    nx, block, _ = first.shape
    count = ny * images
    return pl.pallas_call(
        expert_kernel,
        grid=(nx,),
        in_specs=[
            pl.BlockSpec(rows.shape, lambda i: (0, 0, 0, 0)),
            pl.BlockSpec((1, block, width), lambda i: (i, 0, 0)),
            pl.BlockSpec((1, block, width), lambda i: (i, 0, 0)),
        ],
        out_specs=[
            pl.BlockSpec(rows.shape, lambda i: (0, 0, 0, 0)),
            pl.BlockSpec((1, count, block), lambda i: (i, 0, 0)),
            pl.BlockSpec((1, count, block), lambda i: (i, 0, 0)),
        ],
        out_shape=[
            jax.ShapeDtypeStruct(rows.shape, BF),
            jax.ShapeDtypeStruct((nx, count, block), BF),
            jax.ShapeDtypeStruct((nx, count, block), BF),
        ],
        scratch_shapes=[pltpu.VMEM((count, width), F32), pltpu.VMEM((count, width), F32)],
        compiler_params=pltpu.CompilerParams(vmem_limit_bytes=40 * 1024 * 1024),
        cost_estimate=pl.CostEstimate(
            flops=8 * nx * count * block * width,
            bytes_accessed=4 * rows.size + 4 * first.size + 4 * nx * count * block,
            transcendentals=2 * nx * count * block,
        ),
    )(rows, first, second)


def sum_of_all(local, nx, ny, nz, nc):
    experts, width = local.shape
    plane = nx * ny * nc
    pieces = local.astype(BF).reshape(plane, experts // plane, width)
    mine = exchange(pieces, ("x", "y", "c")).astype(F32).sum(axis=0).astype(BF)
    total = spread(mine, "z", nz).astype(F32).sum(axis=0).astype(BF)
    return spread(total, ("x", "y", "c"), plane).reshape(experts, width).astype(F32)


def per_device(nx, ny, nz, nc, tokens, router, w_in, w_out, out_grad):
    tok, og = tokens[0], out_grad[0]
    width = tok.shape[1]
    experts = nz * nc

    first = lax.all_gather(w_in[0].T, "x", axis=0, tiled=False)
    second = lax.all_gather(w_out[0], "x", axis=0, tiled=False)

    logits = jnp.dot(tok, router, preferred_element_type=F32)
    dispatch = jax.nn.softmax(logits, axis=0)
    combine = jax.nn.softmax(logits, axis=1)
    dispatch_b = dispatch.astype(BF)
    combine_b = combine.astype(BF)
    slots = dot(dispatch_b, tok, ((0,), (0,))).astype(BF)
    slot_grad = dot(combine_b, og, ((0,), (0,))).astype(BF)
    sent = jnp.stack([slots, slot_grad], axis=1)
    mine = exchange(sent, ("z", "c"))
    pair = jnp.stack([mine[:, 0], mine[:, 1]], axis=0)
    rows = spread(pair, "y", ny)

    partial, act, pre_grad = expert_parts(rows, first, second)
    parts_of_mine = exchange(partial, "y")
    rows_in = rows[:, 0].reshape(ny * experts, width)
    rows_grad = rows[:, 1].reshape(ny * experts, width)
    out_part = jnp.einsum("xrf,rd->xfd", act, rows_grad, preferred_element_type=F32)
    in_part = jnp.einsum("xrf,rd->xfd", pre_grad, rows_in, preferred_element_type=F32)
    parts_of_mine, out_part, in_part = lax.optimization_barrier((parts_of_mine, out_part, in_part))
    w_in_grad = lax.psum_scatter(in_part, "x", scatter_dimension=0, tiled=False)
    w_out_grad = lax.psum_scatter(out_part, "x", scatter_dimension=0, tiled=False)

    summed = parts_of_mine.astype(F32).sum(axis=0).astype(BF)
    back = exchange(jnp.stack([summed[0], summed[1]], axis=1), ("z", "c"))
    expert_out, slot_in_grad = back[:, 0], back[:, 1]

    combine_dot = dot(og, expert_out, ((1,), (1,)))
    combine_part = combine * (combine_dot - jnp.sum(combine * combine_dot, axis=1, keepdims=True))
    dispatch_dot = dot(tok, slot_in_grad, ((1,), (1,)))
    dispatch_part = dispatch * (
        dispatch_dot - jnp.sum(dispatch * dispatch_dot, axis=0, keepdims=True)
    )
    logit_grad = (combine_part + dispatch_part).astype(BF)
    router_local = dot(logit_grad, tok, ((0,), (0,)))
    router_grad = sum_of_all(router_local, nx, ny, nz, nc).T
    token_grad = dot(logit_grad, router, ((1,), (1,))) + dot(
        dispatch_b, slot_in_grad, ((1,), (0,))
    )
    return token_grad.astype(BF)[None], router_grad, w_in_grad.T[None], w_out_grad[None]


def solution(mesh):
    dp, expert = mesh.shape["dp"], mesh.shape["expert"]
    nx, ny, nz, nc = 4, dp // 4, expert // 2, 2
    fine = Mesh(np.asarray(mesh.devices).reshape(nx, ny, nz, nc), ALL)

    def run(*args):
        return per_device(nx, ny, nz, nc, *args)

    return jax.shard_map(
        run,
        mesh=fine,
        in_specs=(
            P(ALL, None, None),
            P(),
            P(("z", "c"), None, ("x", "y")),
            P(("z", "c"), ("x", "y"), None),
            P(ALL, None, None),
        ),
        out_specs=(
            P(ALL, None, None),
            P(),
            P(("z", "c"), None, ("x", "y")),
            P(("z", "c"), ("x", "y"), None),
        ),
        check_vma=False,
    )
```

```python
import jax
import jax.numpy as jnp
import numpy as np
from jax import lax
from jax.experimental import pallas as pl
from jax.experimental.pallas import tpu as pltpu
from jax.sharding import Mesh
from jax.sharding import PartitionSpec as P

BF = jnp.bfloat16
F32 = jnp.float32
ALL = ("x", "y", "z", "c")
VMEM_BYTES = 60 * 1024 * 1024


def exchange(parts, axes):
    return lax.all_to_all(parts, axes, split_axis=0, concat_axis=0, tiled=True)


def spread(mine, axes, count):
    return exchange(jnp.broadcast_to(mine[None], (count, *mine.shape)), axes)


def dot(a, b, dims):
    return lax.dot_general(a, b, (dims, ((), ())), preferred_element_type=F32)


def front_kernel(
    tok_ref, router_ref, grad_ref, first_ref, second_ref,
    dispatch_ref, combine_ref, dispatch_b_ref, slots_ref, weights_ref, sems,
):
    block = first_ref.shape[0]
    copies = [
        pltpu.make_async_copy(first_ref, weights_ref.at[pl.ds(0, block)], sems.at[0]),
        pltpu.make_async_copy(second_ref, weights_ref.at[pl.ds(block, block)], sems.at[1]),
    ]
    for copy in copies:
        copy.start()
    tok = tok_ref[...]
    logits = dot(tok, router_ref[...], ((1,), (1,)))
    up = jnp.exp(logits - jnp.max(logits, axis=0, keepdims=True))
    dispatch = up / jnp.sum(up, axis=0, keepdims=True)
    across = jnp.exp(logits - jnp.max(logits, axis=1, keepdims=True))
    combine = across / jnp.sum(across, axis=1, keepdims=True)
    dispatch_ref[...] = dispatch
    combine_ref[...] = combine
    dispatch_b = dispatch.astype(BF)
    dispatch_b_ref[...] = dispatch_b
    slots_ref[0] = dot(dispatch_b, tok, ((0,), (0,))).astype(BF)
    slots_ref[1] = dot(combine.astype(BF), grad_ref[...], ((0,), (0,))).astype(BF)
    for copy in copies:
        copy.wait()


def front(tok, router_t, og, first, second):
    count, width = tok.shape
    experts = router_t.shape[0]
    block = first.shape[0]
    whole = pl.BlockSpec(memory_space=pltpu.VMEM)
    placed = pl.BlockSpec(memory_space=pl.ANY)
    return pl.pallas_call(
        front_kernel,
        in_specs=[whole, whole, whole, placed, placed],
        out_specs=[whole, whole, whole, whole, placed],
        out_shape=[
            jax.ShapeDtypeStruct((count, experts), F32),
            jax.ShapeDtypeStruct((count, experts), F32),
            jax.ShapeDtypeStruct((count, experts), BF),
            jax.ShapeDtypeStruct((2, experts, width), BF),
            jax.ShapeDtypeStruct((2 * block, width), BF),
        ],
        scratch_shapes=[pltpu.SemaphoreType.DMA((2,))],
        compiler_params=pltpu.CompilerParams(vmem_limit_bytes=VMEM_BYTES),
        cost_estimate=pl.CostEstimate(
            flops=6 * count * width * experts,
            bytes_accessed=4 * tok.size + 8 * first.size,
            transcendentals=2 * count * experts,
        ),
    )(tok, router_t, og, first, second)


def expert_kernel(rows_ref, first_ref, second_ref, partial_ref, act_ref, pre_ref, out_sum, in_sum):
    step = pl.program_id(0)
    count, width = out_sum.shape
    rows_in = rows_ref[:, 0].reshape(count, width)
    rows_grad = rows_ref[:, 1].reshape(count, width)
    first, second = first_ref[0], second_ref[0]
    hidden = dot(rows_in, first, ((1,), (1,)))
    act_grad = dot(rows_grad, second, ((1,), (1,)))
    cdf = 0.5 * (1.0 + lax.erf(hidden * 0.7071067811865476))
    slope = cdf + hidden * jnp.exp(-0.5 * hidden * hidden) * 0.3989422804014327
    act = (hidden * cdf).astype(BF)
    pre_grad = (act_grad * slope).astype(BF)
    act_ref[0] = act
    pre_ref[0] = pre_grad
    out_part = dot(act, second, ((1,), (0,)))
    in_part = dot(pre_grad, first, ((1,), (0,)))

    @pl.when(step == 0)
    def _():
        out_sum[...] = out_part
        in_sum[...] = in_part

    @pl.when(step > 0)
    def _():
        out_sum[...] += out_part
        in_sum[...] += in_part

    @pl.when(step == pl.num_programs(0) - 1)
    def _():
        shape = partial_ref.shape[:1] + partial_ref.shape[2:]
        partial_ref[:, 0] = out_sum[...].astype(BF).reshape(shape)
        partial_ref[:, 1] = in_sum[...].astype(BF).reshape(shape)


def expert_parts(rows, weights):
    ny, _, images, width = rows.shape
    nx, double, _ = weights.shape
    block = double // 2
    count = ny * images
    return pl.pallas_call(
        expert_kernel,
        grid=(nx,),
        in_specs=[
            pl.BlockSpec(rows.shape, lambda i: (0, 0, 0, 0)),
            pl.BlockSpec((1, block, width), lambda i: (i, 0, 0)),
            pl.BlockSpec((1, block, width), lambda i: (i, 1, 0)),
        ],
        out_specs=[
            pl.BlockSpec(rows.shape, lambda i: (0, 0, 0, 0)),
            pl.BlockSpec((1, count, block), lambda i: (i, 0, 0)),
            pl.BlockSpec((1, count, block), lambda i: (i, 0, 0)),
        ],
        out_shape=[
            jax.ShapeDtypeStruct(rows.shape, BF),
            jax.ShapeDtypeStruct((nx, count, block), BF),
            jax.ShapeDtypeStruct((nx, count, block), BF),
        ],
        scratch_shapes=[pltpu.VMEM((count, width), F32), pltpu.VMEM((count, width), F32)],
        compiler_params=pltpu.CompilerParams(vmem_limit_bytes=VMEM_BYTES),
        cost_estimate=pl.CostEstimate(
            flops=8 * nx * count * block * width,
            bytes_accessed=4 * rows.size + 2 * weights.size + 4 * nx * count * block,
            transcendentals=2 * nx * count * block,
        ),
    )(rows, weights, weights)


def weight_kernel(rows_ref, act_ref, pre_ref, parts_ref):
    ny, _, images, width = rows_ref.shape
    block = act_ref.shape[2]
    rows_in = rows_ref[:, 0].reshape(ny * images, width)
    rows_grad = rows_ref[:, 1].reshape(ny * images, width)
    parts_ref[0, :block] = dot(pre_ref[0], rows_in, ((0,), (0,))).astype(BF)
    parts_ref[0, block:] = dot(act_ref[0], rows_grad, ((0,), (0,))).astype(BF)


def weight_parts(rows, act, pre_grad):
    nx, count, block = act.shape
    width = rows.shape[3]
    return pl.pallas_call(
        weight_kernel,
        grid=(nx,),
        in_specs=[
            pl.BlockSpec(rows.shape, lambda i: (0, 0, 0, 0)),
            pl.BlockSpec((1, count, block), lambda i: (i, 0, 0)),
            pl.BlockSpec((1, count, block), lambda i: (i, 0, 0)),
        ],
        out_specs=pl.BlockSpec((1, 2 * block, width), lambda i: (i, 0, 0)),
        out_shape=jax.ShapeDtypeStruct((nx, 2 * block, width), BF),
        compiler_params=pltpu.CompilerParams(vmem_limit_bytes=VMEM_BYTES),
        cost_estimate=pl.CostEstimate(
            flops=4 * nx * count * block * width,
            bytes_accessed=2 * rows.size + 4 * act.size + 4 * nx * block * width,
            transcendentals=0,
        ),
    )(rows, act, pre_grad)


def per_device(nx, ny, nz, nc, tokens, router, w_in, w_out, out_grad):
    tok, og = tokens[0], out_grad[0]
    width = tok.shape[1]
    experts = nz * nc
    block = w_out.shape[1]
    plane = nx * ny * nc

    dispatch, combine, dispatch_b, slots, weights = front(tok, router.T, og, w_in[0].T, w_out[0])
    gathered = lax.all_gather(weights, "x", axis=0, tiled=False)
    mine = exchange(jnp.stack([slots[0], slots[1]], axis=1), ("z", "c"))
    rows = spread(jnp.stack([mine[:, 0], mine[:, 1]], axis=0), "y", ny)

    partial, act, pre_grad = expert_parts(rows, gathered)
    parts_of_mine = exchange(partial, "y")
    parts = weight_parts(rows, act, pre_grad)
    parts_of_mine, parts = lax.optimization_barrier((parts_of_mine, parts))
    grads = lax.psum_scatter(parts, "x", scatter_dimension=0, tiled=False)

    summed = parts_of_mine.astype(F32).sum(axis=0).astype(BF)
    back = exchange(jnp.stack([summed[0], summed[1]], axis=1), ("z", "c"))
    expert_out, slot_in_grad = back[:, 0], back[:, 1]

    combine_dot = dot(og, expert_out, ((1,), (1,)))
    combine_part = combine * (combine_dot - jnp.sum(combine * combine_dot, axis=1, keepdims=True))
    dispatch_dot = dot(tok, slot_in_grad, ((1,), (1,)))
    dispatch_part = dispatch * (
        dispatch_dot - jnp.sum(dispatch * dispatch_dot, axis=0, keepdims=True)
    )
    logit_grad = (combine_part + dispatch_part).astype(BF)

    local = dot(logit_grad, tok, ((0,), (0,))).astype(BF)
    pieces = exchange(local.reshape(plane, experts // plane, width), ("x", "y", "c"))
    piece = pieces.astype(F32).sum(axis=0).astype(BF)
    piece, grads, logit_grad = lax.optimization_barrier((piece, grads, logit_grad))
    along_z = spread(piece, "z", nz)
    w_in_grad = grads[:block].astype(F32)
    w_out_grad = grads[block:].astype(F32)
    token_grad = dot(logit_grad, router, ((1,), (1,))) + dot(
        dispatch_b, slot_in_grad, ((1,), (0,))
    )
    token_grad = token_grad.astype(BF)
    along_z, w_in_grad, w_out_grad, token_grad = lax.optimization_barrier(
        (along_z, w_in_grad, w_out_grad, token_grad)
    )
    total = along_z.astype(F32).sum(axis=0).astype(BF)
    router_grad = spread(total, ("x", "y", "c"), plane).reshape(experts, width).astype(F32).T
    return token_grad[None], router_grad, w_in_grad.T[None], w_out_grad[None]


def solution(mesh):
    dp, expert = mesh.shape["dp"], mesh.shape["expert"]
    nx, ny, nz, nc = 4, dp // 4, expert // 2, 2
    fine = Mesh(np.asarray(mesh.devices).reshape(nx, ny, nz, nc), ALL)

    def run(*args):
        return per_device(nx, ny, nz, nc, *args)

    return jax.shard_map(
        run,
        mesh=fine,
        in_specs=(
            P(ALL, None, None),
            P(),
            P(("z", "c"), None, ("x", "y")),
            P(("z", "c"), ("x", "y"), None),
            P(ALL, None, None),
        ),
        out_specs=(
            P(ALL, None, None),
            P(),
            P(("z", "c"), None, ("x", "y")),
            P(("z", "c"), ("x", "y"), None),
        ),
        check_vma=False,
    )
```

```python
import jax
import jax.numpy as jnp
import numpy as np
from jax import lax
from jax.experimental import pallas as pl
from jax.experimental.pallas import tpu as pltpu
from jax.sharding import Mesh
from jax.sharding import PartitionSpec as P

BF = jnp.bfloat16
F32 = jnp.float32
ALL = ("x", "y", "z", "c")
VMEM_BYTES = 16 * 1024 * 1024


def exchange(parts, axes):
    return lax.all_to_all(parts, axes, split_axis=0, concat_axis=0, tiled=True)


def spread(mine, axes, count):
    return exchange(jnp.broadcast_to(mine[None], (count, *mine.shape)), axes)


def dot(a, b, dims):
    return lax.dot_general(a, b, (dims, ((), ())), preferred_element_type=F32)


def gelu_exact(value):
    return 0.5 * value * (1.0 + jax.scipy.special.erf(value * 0.7071067811865476))


def gelu_slope(value):
    return (
        0.5 * (1.0 + jax.scipy.special.erf(value * 0.7071067811865476))
        + value * jnp.exp(-0.5 * value * value) * 0.3989422804014327
    )


def weight_kernel(rows_in_ref, rows_grad_ref, act_ref, pre_ref, parts_ref):
    nx, double, _ = parts_ref.shape
    block = double // 2
    in_part = dot(pre_ref[...], rows_in_ref[...], ((0,), (0,))).astype(BF)
    out_part = dot(act_ref[...], rows_grad_ref[...], ((0,), (0,))).astype(BF)
    for i in range(nx):
        parts_ref[i, :block] = in_part[i * block : (i + 1) * block]
        parts_ref[i, block:] = out_part[i * block : (i + 1) * block]


def weight_parts(rows_in, rows_grad, act, pre_grad, nx):
    count, units = act.shape
    width = rows_in.shape[1]
    block = units // nx
    tile = min(256, width)
    columns = pl.BlockSpec((count, tile), lambda i: (0, i))
    whole = pl.BlockSpec((count, units), lambda i: (0, 0))
    return pl.pallas_call(
        weight_kernel,
        grid=(width // tile,),
        in_specs=[columns, columns, whole, whole],
        out_specs=pl.BlockSpec((nx, 2 * block, tile), lambda i: (0, 0, i)),
        out_shape=jax.ShapeDtypeStruct((nx, 2 * block, width), BF),
        compiler_params=pltpu.CompilerParams(vmem_limit_bytes=VMEM_BYTES),
        cost_estimate=pl.CostEstimate(
            flops=4 * count * units * width,
            bytes_accessed=4 * rows_in.size + 4 * act.size + 4 * units * width,
            transcendentals=0,
        ),
    )(rows_in, rows_grad, act, pre_grad)


def per_device(nx, ny, nz, nc, tokens, router, w_in, w_out, out_grad):
    tok, og = tokens[0], out_grad[0]
    width = tok.shape[1]
    experts = nz * nc
    block = w_out.shape[1]
    plane = nx * ny * nc

    weights = jnp.concatenate([w_in[0].T, w_out[0]], axis=0)
    gathered = lax.all_gather(weights, "x", axis=0, tiled=False)

    logits = jnp.dot(tok, router, preferred_element_type=F32)
    dispatch = jax.nn.softmax(logits, axis=0)
    combine = jax.nn.softmax(logits, axis=1)
    dispatch_b = dispatch.astype(BF)
    combine_b = combine.astype(BF)
    slots = dot(dispatch_b, tok, ((0,), (0,))).astype(BF)
    slot_grad = dot(combine_b, og, ((0,), (0,))).astype(BF)
    mine = exchange(jnp.stack([slots, slot_grad], axis=1), ("z", "c"))
    rows = spread(jnp.stack([mine[:, 0], mine[:, 1]], axis=0), "y", ny)
    first = gathered[:, :block].reshape(nx * block, width)
    second = gathered[:, block:].reshape(nx * block, width)
    rows, first, second = lax.optimization_barrier((rows, first, second))
    rows_in = rows[:, 0].reshape(ny * experts, width)
    rows_grad = rows[:, 1].reshape(ny * experts, width)

    hidden = dot(rows_in, first, ((1,), (1,)))
    act = gelu_exact(hidden).astype(BF)
    act_grad = dot(rows_grad, second, ((1,), (1,)))
    pre_grad = (act_grad * gelu_slope(hidden)).astype(BF)
    partial_out = dot(act, second, ((1,), (0,))).astype(BF)
    partial_in = dot(pre_grad, first, ((1,), (0,))).astype(BF)
    partial = jnp.stack(
        [partial_out.reshape(ny, experts, width), partial_in.reshape(ny, experts, width)], axis=1
    )
    parts_of_mine = exchange(partial, "y")
    parts = weight_parts(rows_in, rows_grad, act, pre_grad, nx)
    parts_of_mine, parts = lax.optimization_barrier((parts_of_mine, parts))
    grads = lax.psum_scatter(parts, "x", scatter_dimension=0, tiled=False)

    summed = parts_of_mine.astype(F32).sum(axis=0).astype(BF)
    back = exchange(jnp.stack([summed[0], summed[1]], axis=1), ("z", "c"))
    expert_out, slot_in_grad = back[:, 0], back[:, 1]

    combine_dot = dot(og, expert_out, ((1,), (1,)))
    combine_part = combine * (combine_dot - jnp.sum(combine * combine_dot, axis=1, keepdims=True))
    dispatch_dot = dot(tok, slot_in_grad, ((1,), (1,)))
    dispatch_part = dispatch * (
        dispatch_dot - jnp.sum(dispatch * dispatch_dot, axis=0, keepdims=True)
    )
    logit_grad = (combine_part + dispatch_part).astype(BF)

    local = dot(logit_grad, tok, ((0,), (0,))).astype(BF)
    pieces = exchange(local.reshape(plane, experts // plane, width), ("x", "y", "c"))
    piece = pieces.astype(F32).sum(axis=0).astype(BF)
    piece, grads, logit_grad = lax.optimization_barrier((piece, grads, logit_grad))
    along_z = spread(piece, "z", nz)
    w_in_grad = grads[:block].astype(F32)
    w_out_grad = grads[block:].astype(F32)
    token_grad = dot(logit_grad, router, ((1,), (1,))) + dot(
        dispatch_b, slot_in_grad, ((1,), (0,))
    )
    token_grad = token_grad.astype(BF)
    along_z, w_in_grad, w_out_grad, token_grad = lax.optimization_barrier(
        (along_z, w_in_grad, w_out_grad, token_grad)
    )
    total = along_z.astype(F32).sum(axis=0).astype(BF)
    router_grad = spread(total, ("x", "y", "c"), plane).reshape(experts, width).astype(F32).T
    return token_grad[None], router_grad, w_in_grad.T[None], w_out_grad[None]


def solution(mesh):
    dp, expert = mesh.shape["dp"], mesh.shape["expert"]
    nx, ny, nz, nc = 4, dp // 4, expert // 2, 2
    fine = Mesh(np.asarray(mesh.devices).reshape(nx, ny, nz, nc), ALL)

    def run(*args):
        return per_device(nx, ny, nz, nc, *args)

    return jax.shard_map(
        run,
        mesh=fine,
        in_specs=(
            P(ALL, None, None),
            P(),
            P(("z", "c"), None, ("x", "y")),
            P(("z", "c"), ("x", "y"), None),
            P(ALL, None, None),
        ),
        out_specs=(
            P(ALL, None, None),
            P(),
            P(("z", "c"), None, ("x", "y")),
            P(("z", "c"), ("x", "y"), None),
        ),
        check_vma=False,
    )
```

```python
import jax
import jax.numpy as jnp
import numpy as np
from jax import lax
from jax.experimental import pallas as pl
from jax.experimental.pallas import tpu as pltpu
from jax.sharding import Mesh
from jax.sharding import PartitionSpec as P

BF = jnp.bfloat16
F32 = jnp.float32
ALL = ("x", "y", "z", "c")
VMEM_BYTES = 16 * 1024 * 1024


def exchange(parts, axes):
    return lax.all_to_all(parts, axes, split_axis=0, concat_axis=0, tiled=True)


def spread(mine, axes, count):
    return exchange(jnp.broadcast_to(mine[None], (count, *mine.shape)), axes)


def dot(a, b, dims):
    return lax.dot_general(a, b, (dims, ((), ())), preferred_element_type=F32)


def gelu_exact(value):
    return 0.5 * value * (1.0 + jax.scipy.special.erf(value * 0.7071067811865476))


def gelu_slope(value):
    return (
        0.5 * (1.0 + jax.scipy.special.erf(value * 0.7071067811865476))
        + value * jnp.exp(-0.5 * value * value) * 0.3989422804014327
    )


def weight_kernel(rows_in_ref, rows_grad_ref, act_ref, pre_ref, parts_ref):
    nx, double, _ = parts_ref.shape
    block = double // 2
    in_part = dot(pre_ref[...], rows_in_ref[...], ((0,), (0,))).astype(BF)
    out_part = dot(act_ref[...], rows_grad_ref[...], ((0,), (0,))).astype(BF)
    for i in range(nx):
        parts_ref[i, :block] = in_part[i * block : (i + 1) * block]
        parts_ref[i, block:] = out_part[i * block : (i + 1) * block]


def weight_parts(rows_in, rows_grad, act, pre_grad, nx):
    count, units = act.shape
    width = rows_in.shape[1]
    block = units // nx
    tile = min(256, width)
    columns = pl.BlockSpec((count, tile), lambda i: (0, i))
    whole = pl.BlockSpec((count, units), lambda i: (0, 0))
    return pl.pallas_call(
        weight_kernel,
        grid=(width // tile,),
        in_specs=[columns, columns, whole, whole],
        out_specs=pl.BlockSpec((nx, 2 * block, tile), lambda i: (0, 0, i)),
        out_shape=jax.ShapeDtypeStruct((nx, 2 * block, width), BF),
        compiler_params=pltpu.CompilerParams(vmem_limit_bytes=VMEM_BYTES),
        cost_estimate=pl.CostEstimate(
            flops=4 * count * units * width,
            bytes_accessed=4 * rows_in.size + 4 * act.size + 4 * units * width,
            transcendentals=0,
        ),
    )(rows_in, rows_grad, act, pre_grad)


def per_device(nx, ny, nz, nc, tokens, router, w_in, w_out, out_grad):
    tok, og = tokens[0], out_grad[0]
    width = tok.shape[1]
    experts = nz * nc
    block = w_out.shape[1]
    plane = nx * ny * nc

    weights = jnp.concatenate([w_in[0].T, w_out[0]], axis=0)
    gathered = lax.all_gather(weights, "x", axis=0, tiled=False)

    logits = jnp.dot(tok, router, preferred_element_type=F32)
    dispatch = jax.nn.softmax(logits, axis=0)
    combine = jax.nn.softmax(logits, axis=1)
    dispatch_b = dispatch.astype(BF)
    combine_b = combine.astype(BF)
    slots = dot(dispatch_b, tok, ((0,), (0,))).astype(BF)
    slot_grad = dot(combine_b, og, ((0,), (0,))).astype(BF)
    sent = jnp.stack([slots, slot_grad], axis=1).reshape(nz, nc * 2, width)
    mine = exchange(sent, "z").reshape(nz, nc, 2, width).transpose(1, 2, 0, 3)
    copies = jnp.broadcast_to(mine[None], (ny, nc, 2, nz, width))
    rows = exchange(copies.reshape(ny * nc, 2, nz, width), ("y", "c"))
    first = gathered[:, :block].reshape(nx * block, width)
    second = gathered[:, block:].reshape(nx * block, width)
    rows, first, second = lax.optimization_barrier((rows, first, second))
    rows_in = rows[:, 0].reshape(ny * experts, width)
    rows_grad = rows[:, 1].reshape(ny * experts, width)

    hidden = dot(rows_in, first, ((1,), (1,)))
    act = gelu_exact(hidden).astype(BF)
    act_grad = dot(rows_grad, second, ((1,), (1,)))
    pre_grad = (act_grad * gelu_slope(hidden)).astype(BF)
    partial_out = dot(act, second, ((1,), (0,))).astype(BF)
    partial_in = dot(pre_grad, first, ((1,), (0,))).astype(BF)
    shape = (ny * nc, nz, width)
    partial = jnp.stack([partial_out.reshape(shape), partial_in.reshape(shape)], axis=1)
    parts_of_mine = exchange(partial, ("y", "c"))
    parts = weight_parts(rows_in, rows_grad, act, pre_grad, nx)
    parts_of_mine, parts = lax.optimization_barrier((parts_of_mine, parts))
    grads = lax.psum_scatter(parts, "x", scatter_dimension=0, tiled=False)

    summed = parts_of_mine.reshape(ny, nc, 2, nz, width).astype(F32).sum(axis=0).astype(BF)
    back = exchange(summed.transpose(2, 0, 1, 3).reshape(nz, nc * 2, width), "z")
    back = back.reshape(experts, 2, width)
    expert_out, slot_in_grad = back[:, 0], back[:, 1]

    combine_dot = dot(og, expert_out, ((1,), (1,)))
    combine_part = combine * (combine_dot - jnp.sum(combine * combine_dot, axis=1, keepdims=True))
    dispatch_dot = dot(tok, slot_in_grad, ((1,), (1,)))
    dispatch_part = dispatch * (
        dispatch_dot - jnp.sum(dispatch * dispatch_dot, axis=0, keepdims=True)
    )
    logit_grad = (combine_part + dispatch_part).astype(BF)

    local = dot(logit_grad, tok, ((0,), (0,))).astype(BF)
    pieces = exchange(local.reshape(plane, experts // plane, width), ("x", "y", "c"))
    piece = pieces.astype(F32).sum(axis=0).astype(BF)
    piece, grads, logit_grad = lax.optimization_barrier((piece, grads, logit_grad))
    along_z = spread(piece, "z", nz)
    w_in_grad = grads[:block].astype(F32)
    w_out_grad = grads[block:].astype(F32)
    token_grad = dot(logit_grad, router, ((1,), (1,))) + dot(
        dispatch_b, slot_in_grad, ((1,), (0,))
    )
    token_grad = token_grad.astype(BF)
    along_z, w_in_grad, w_out_grad, token_grad = lax.optimization_barrier(
        (along_z, w_in_grad, w_out_grad, token_grad)
    )
    total = along_z.astype(F32).sum(axis=0).astype(BF)
    router_grad = spread(total, ("x", "y", "c"), plane).reshape(experts, width).astype(F32).T
    return token_grad[None], router_grad, w_in_grad.T[None], w_out_grad[None]


def solution(mesh):
    dp, expert = mesh.shape["dp"], mesh.shape["expert"]
    nx, ny, nz, nc = 4, dp // 4, expert // 2, 2
    fine = Mesh(np.asarray(mesh.devices).reshape(nx, ny, nz, nc), ALL)

    def run(*args):
        return per_device(nx, ny, nz, nc, *args)

    return jax.shard_map(
        run,
        mesh=fine,
        in_specs=(
            P(ALL, None, None),
            P(),
            P(("z", "c"), None, ("x", "y")),
            P(("z", "c"), ("x", "y"), None),
            P(ALL, None, None),
        ),
        out_specs=(
            P(ALL, None, None),
            P(),
            P(("z", "c"), None, ("x", "y")),
            P(("z", "c"), ("x", "y"), None),
        ),
        check_vma=False,
    )
```

```python
import jax
import jax.numpy as jnp
import numpy as np
from jax import lax
from jax.experimental import pallas as pl
from jax.experimental.pallas import tpu as pltpu
from jax.sharding import Mesh
from jax.sharding import PartitionSpec as P

BF = jnp.bfloat16
F32 = jnp.float32
Z = ("zh", "zl")
ALL = ("x", "y", "zh", "zl", "c")
EXPERT = ("zh", "zl", "c")
BOX = ("x", "y", "zl", "c")
VMEM_BYTES = 16 * 1024 * 1024


def exchange(parts, axes):
    return lax.all_to_all(parts, axes, split_axis=0, concat_axis=0, tiled=True)


def spread(mine, axes, count):
    return exchange(jnp.broadcast_to(mine[None], (count, *mine.shape)), axes)


def dot(a, b, dims):
    return lax.dot_general(a, b, (dims, ((), ())), preferred_element_type=F32)


def gelu_exact(value):
    return 0.5 * value * (1.0 + jax.scipy.special.erf(value * 0.7071067811865476))


def gelu_slope(value):
    return (
        0.5 * (1.0 + jax.scipy.special.erf(value * 0.7071067811865476))
        + value * jnp.exp(-0.5 * value * value) * 0.3989422804014327
    )


def weight_kernel(rows_in_ref, rows_grad_ref, act_ref, pre_ref, parts_ref):
    nx, double, _ = parts_ref.shape
    block = double // 2
    in_part = dot(pre_ref[...], rows_in_ref[...], ((0,), (0,))).astype(BF)
    out_part = dot(act_ref[...], rows_grad_ref[...], ((0,), (0,))).astype(BF)
    for i in range(nx):
        parts_ref[i, :block] = in_part[i * block : (i + 1) * block]
        parts_ref[i, block:] = out_part[i * block : (i + 1) * block]


def weight_parts(rows_in, rows_grad, act, pre_grad, nx):
    count, units = act.shape
    width = rows_in.shape[1]
    block = units // nx
    tile = min(256, width)
    columns = pl.BlockSpec((count, tile), lambda i: (0, i))
    whole = pl.BlockSpec((count, units), lambda i: (0, 0))
    return pl.pallas_call(
        weight_kernel,
        grid=(width // tile,),
        in_specs=[columns, columns, whole, whole],
        out_specs=pl.BlockSpec((nx, 2 * block, tile), lambda i: (0, 0, i)),
        out_shape=jax.ShapeDtypeStruct((nx, 2 * block, width), BF),
        compiler_params=pltpu.CompilerParams(vmem_limit_bytes=VMEM_BYTES),
        cost_estimate=pl.CostEstimate(
            flops=4 * count * units * width,
            bytes_accessed=4 * rows_in.size + 4 * act.size + 4 * units * width,
            transcendentals=0,
        ),
    )(rows_in, rows_grad, act, pre_grad)


def per_device(nx, ny, nz, nl, nc, tokens, router, w_in, w_out, out_grad):
    tok, og = tokens[0], out_grad[0]
    width = tok.shape[1]
    experts = nz * nc
    block = w_out.shape[1]
    box = nx * ny * nl * nc

    weights = jnp.concatenate([w_in[0].T, w_out[0]], axis=0)
    gathered = lax.all_gather(weights, "x", axis=0, tiled=False)

    logits = jnp.dot(tok, router, preferred_element_type=F32)
    dispatch = jax.nn.softmax(logits, axis=0)
    combine = jax.nn.softmax(logits, axis=1)
    dispatch_b = dispatch.astype(BF)
    combine_b = combine.astype(BF)
    slots = dot(dispatch_b, tok, ((0,), (0,))).astype(BF)
    slot_grad = dot(combine_b, og, ((0,), (0,))).astype(BF)
    sent = jnp.stack([slots, slot_grad], axis=1).reshape(nz, nc * 2, width)
    mine = exchange(sent, Z).reshape(nz, nc, 2, width).transpose(1, 2, 0, 3)
    copies = jnp.broadcast_to(mine[None], (ny, nc, 2, nz, width))
    rows = exchange(copies.reshape(ny * nc, 2, nz, width), ("y", "c"))
    first = gathered[:, :block].reshape(nx * block, width)
    second = gathered[:, block:].reshape(nx * block, width)
    rows, first, second = lax.optimization_barrier((rows, first, second))
    rows_in = rows[:, 0].reshape(ny * experts, width)
    rows_grad = rows[:, 1].reshape(ny * experts, width)

    hidden = dot(rows_in, first, ((1,), (1,)))
    act = gelu_exact(hidden).astype(BF)
    act_grad = dot(rows_grad, second, ((1,), (1,)))
    pre_grad = (act_grad * gelu_slope(hidden)).astype(BF)
    partial_out = dot(act, second, ((1,), (0,))).astype(BF)
    partial_in = dot(pre_grad, first, ((1,), (0,))).astype(BF)
    shape = (ny * nc, nz, width)
    partial = jnp.stack([partial_out.reshape(shape), partial_in.reshape(shape)], axis=1)
    parts_of_mine = exchange(partial, ("y", "c"))
    parts = weight_parts(rows_in, rows_grad, act, pre_grad, nx)
    parts_of_mine, parts = lax.optimization_barrier((parts_of_mine, parts))
    grads = lax.psum_scatter(parts, "x", scatter_dimension=0, tiled=False)

    summed = parts_of_mine.reshape(ny, nc, 2, nz, width).astype(F32).sum(axis=0).astype(BF)
    back = exchange(summed.transpose(2, 0, 1, 3).reshape(nz, nc * 2, width), Z)
    back = back.reshape(experts, 2, width)
    expert_out, slot_in_grad = back[:, 0], back[:, 1]

    combine_dot = dot(og, expert_out, ((1,), (1,)))
    combine_part = combine * (combine_dot - jnp.sum(combine * combine_dot, axis=1, keepdims=True))
    dispatch_dot = dot(tok, slot_in_grad, ((1,), (1,)))
    dispatch_part = dispatch * (
        dispatch_dot - jnp.sum(dispatch * dispatch_dot, axis=0, keepdims=True)
    )
    logit_grad = (combine_part + dispatch_part).astype(BF)

    local = dot(logit_grad, tok, ((0,), (0,))).astype(BF)
    pieces = exchange(local.reshape(box, 2, -1), BOX)
    piece = pieces.astype(F32).sum(axis=0).astype(BF)
    piece, grads, logit_grad = lax.optimization_barrier((piece, grads, logit_grad))
    along_z = spread(piece, "zh", nz // nl)
    w_in_grad = grads[:block].astype(F32)
    w_out_grad = grads[block:].astype(F32)
    token_grad = dot(logit_grad, router, ((1,), (1,))) + dot(
        dispatch_b, slot_in_grad, ((1,), (0,))
    )
    token_grad = token_grad.astype(BF)
    along_z, w_in_grad, w_out_grad, token_grad = lax.optimization_barrier(
        (along_z, w_in_grad, w_out_grad, token_grad)
    )
    total = along_z.astype(F32).sum(axis=0).astype(BF)
    router_grad = spread(total, BOX, box).reshape(experts, width).astype(F32).T
    return token_grad[None], router_grad, w_in_grad.T[None], w_out_grad[None]


def solution(mesh):
    dp, expert = mesh.shape["dp"], mesh.shape["expert"]
    nx, ny, nz, nl, nc = 4, dp // 4, expert // 2, 2, 2
    fine = Mesh(np.asarray(mesh.devices).reshape(nx, ny, nz // nl, nl, nc), ALL)

    def run(*args):
        return per_device(nx, ny, nz, nl, nc, *args)

    return jax.shard_map(
        run,
        mesh=fine,
        in_specs=(
            P(ALL, None, None),
            P(),
            P(EXPERT, None, ("x", "y")),
            P(EXPERT, ("x", "y"), None),
            P(ALL, None, None),
        ),
        out_specs=(
            P(ALL, None, None),
            P(),
            P(EXPERT, None, ("x", "y")),
            P(EXPERT, ("x", "y"), None),
        ),
        check_vma=False,
    )
```

```python
import jax
import jax.numpy as jnp
import numpy as np
from jax import lax
from jax.experimental import pallas as pl
from jax.experimental.pallas import tpu as pltpu
from jax.sharding import Mesh
from jax.sharding import PartitionSpec as P

BF = jnp.bfloat16
F32 = jnp.float32
Z = ("zh", "zl")
ALL = ("x", "y", "zh", "zl", "c")
EXPERT = ("zh", "zl", "c")
BOX = ("x", "y", "zl", "c")
CHIPS = ("x", "y", "c")
VMEM_BYTES = 16 * 1024 * 1024


def exchange(parts, axes, groups=None):
    return lax.all_to_all(
        parts, axes, split_axis=0, concat_axis=0, tiled=True, axis_index_groups=groups
    )


def spread(mine, axes, count):
    return exchange(jnp.broadcast_to(mine[None], (count, *mine.shape)), axes)


def dot(a, b, dims):
    return lax.dot_general(a, b, (dims, ((), ())), preferred_element_type=F32)


def gelu_exact(value):
    return 0.5 * value * (1.0 + jax.scipy.special.erf(value * 0.7071067811865476))


def gelu_slope(value):
    return (
        0.5 * (1.0 + jax.scipy.special.erf(value * 0.7071067811865476))
        + value * jnp.exp(-0.5 * value * value) * 0.3989422804014327
    )


def weight_kernel(rows_in_ref, rows_grad_ref, act_ref, pre_ref, parts_ref):
    nx, double, _ = parts_ref.shape
    block = double // 2
    in_part = dot(pre_ref[...], rows_in_ref[...], ((0,), (0,))).astype(BF)
    out_part = dot(act_ref[...], rows_grad_ref[...], ((0,), (0,))).astype(BF)
    for i in range(nx):
        parts_ref[i, :block] = in_part[i * block : (i + 1) * block]
        parts_ref[i, block:] = out_part[i * block : (i + 1) * block]


def weight_parts(rows_in, rows_grad, act, pre_grad, nx):
    count, units = act.shape
    width = rows_in.shape[1]
    block = units // nx
    tile = min(256, width)
    columns = pl.BlockSpec((count, tile), lambda i: (0, i))
    whole = pl.BlockSpec((count, units), lambda i: (0, 0))
    return pl.pallas_call(
        weight_kernel,
        grid=(width // tile,),
        in_specs=[columns, columns, whole, whole],
        out_specs=pl.BlockSpec((nx, 2 * block, tile), lambda i: (0, 0, i)),
        out_shape=jax.ShapeDtypeStruct((nx, 2 * block, width), BF),
        compiler_params=pltpu.CompilerParams(vmem_limit_bytes=VMEM_BYTES),
        cost_estimate=pl.CostEstimate(
            flops=4 * count * units * width,
            bytes_accessed=4 * rows_in.size + 4 * act.size + 4 * units * width,
            transcendentals=0,
        ),
    )(rows_in, rows_grad, act, pre_grad)


def per_device(nx, ny, nz, nl, nc, tokens, router, w_in, w_out, out_grad):
    tok, og = tokens[0], out_grad[0]
    width = tok.shape[1]
    experts = nz * nc
    block = w_out.shape[1]
    box = nx * ny * nl * nc

    at = np.arange(nx * ny * nc).reshape(nx, ny, nc)
    row_groups = [*at[:, :, 0].tolist(), *at[:, :, 1].T.tolist()]
    unit_groups = [*at[:, :, 0].T.tolist(), *at[:, :, 1].tolist()]

    weights = jnp.concatenate([w_in[0].T, w_out[0]], axis=0)
    gathered = lax.all_gather(weights, CHIPS, axis=0, tiled=False, axis_index_groups=unit_groups)

    logits = jnp.dot(tok, router, preferred_element_type=F32)
    dispatch = jax.nn.softmax(logits, axis=0)
    combine = jax.nn.softmax(logits, axis=1)
    dispatch_b = dispatch.astype(BF)
    combine_b = combine.astype(BF)
    slots = dot(dispatch_b, tok, ((0,), (0,))).astype(BF)
    slot_grad = dot(combine_b, og, ((0,), (0,))).astype(BF)
    mine = exchange(jnp.stack([slots, slot_grad], axis=1), EXPERT)
    pair = jnp.stack([mine[:, 0], mine[:, 1]], axis=0)
    rows = exchange(jnp.broadcast_to(pair[None], (ny, *pair.shape)), CHIPS, row_groups)
    first = gathered[:, :block].reshape(nx * block, width)
    second = gathered[:, block:].reshape(nx * block, width)
    rows, first, second = lax.optimization_barrier((rows, first, second))
    rows_in = rows[:, 0].reshape(ny * experts, width)
    rows_grad = rows[:, 1].reshape(ny * experts, width)

    hidden = dot(rows_in, first, ((1,), (1,)))
    act = gelu_exact(hidden).astype(BF)
    act_grad = dot(rows_grad, second, ((1,), (1,)))
    pre_grad = (act_grad * gelu_slope(hidden)).astype(BF)
    partial_out = dot(act, second, ((1,), (0,))).astype(BF)
    partial_in = dot(pre_grad, first, ((1,), (0,))).astype(BF)
    shape = (ny, experts, width)
    partial = jnp.stack([partial_out.reshape(shape), partial_in.reshape(shape)], axis=1)
    parts_of_mine = exchange(partial, CHIPS, row_groups)
    parts = weight_parts(rows_in, rows_grad, act, pre_grad, nx)
    parts_of_mine, parts = lax.optimization_barrier((parts_of_mine, parts))
    grads = lax.psum_scatter(
        parts, CHIPS, scatter_dimension=0, tiled=False, axis_index_groups=unit_groups
    )

    summed = parts_of_mine.astype(F32).sum(axis=0).astype(BF)
    back = exchange(jnp.stack([summed[0], summed[1]], axis=1), EXPERT)
    expert_out, slot_in_grad = back[:, 0], back[:, 1]

    combine_dot = dot(og, expert_out, ((1,), (1,)))
    combine_part = combine * (combine_dot - jnp.sum(combine * combine_dot, axis=1, keepdims=True))
    dispatch_dot = dot(tok, slot_in_grad, ((1,), (1,)))
    dispatch_part = dispatch * (
        dispatch_dot - jnp.sum(dispatch * dispatch_dot, axis=0, keepdims=True)
    )
    logit_grad = (combine_part + dispatch_part).astype(BF)

    local = dot(logit_grad, tok, ((0,), (0,))).astype(BF)
    pieces = exchange(local.reshape(box, 2, -1), BOX)
    piece = pieces.astype(F32).sum(axis=0).astype(BF)
    piece, grads, logit_grad = lax.optimization_barrier((piece, grads, logit_grad))
    along_z = spread(piece, "zh", nz // nl)
    w_in_grad = grads[:block].astype(F32)
    w_out_grad = grads[block:].astype(F32)
    token_grad = dot(logit_grad, router, ((1,), (1,))) + dot(
        dispatch_b, slot_in_grad, ((1,), (0,))
    )
    token_grad = token_grad.astype(BF)
    along_z, w_in_grad, w_out_grad, token_grad = lax.optimization_barrier(
        (along_z, w_in_grad, w_out_grad, token_grad)
    )
    total = along_z.astype(F32).sum(axis=0).astype(BF)
    router_grad = spread(total, BOX, box).reshape(experts, width).astype(F32).T
    return token_grad[None], router_grad, w_in_grad.T[None], w_out_grad[None]


def solution(mesh):
    dp, expert = mesh.shape["dp"], mesh.shape["expert"]
    nx, ny, nz, nl, nc = 4, dp // 4, expert // 2, 2, 2
    fine = Mesh(np.asarray(mesh.devices).reshape(nx, ny, nz // nl, nl, nc), ALL)

    def run(*args):
        return per_device(nx, ny, nz, nl, nc, *args)

    return jax.shard_map(
        run,
        mesh=fine,
        in_specs=(
            P(ALL, None, None),
            P(),
            P(EXPERT, None, ("x", "y")),
            P(EXPERT, ("x", "y"), None),
            P(ALL, None, None),
        ),
        out_specs=(
            P(ALL, None, None),
            P(),
            P(EXPERT, None, ("x", "y")),
            P(EXPERT, ("x", "y"), None),
        ),
        check_vma=False,
    )
```

```python
import jax
import jax.numpy as jnp
import numpy as np
from jax import lax
from jax.experimental import pallas as pl
from jax.experimental.pallas import tpu as pltpu
from jax.sharding import Mesh
from jax.sharding import PartitionSpec as P

BF = jnp.bfloat16
F32 = jnp.float32
Z = ("zh", "zl")
ALL = ("x", "y", "zh", "zl", "c")
EXPERT = ("zh", "zl", "c")
BOX = ("x", "y", "zl", "c")
CHIPS = ("x", "y", "c")
VMEM_BYTES = 16 * 1024 * 1024


def exchange(parts, axes, groups=None):
    return lax.all_to_all(
        parts, axes, split_axis=0, concat_axis=0, tiled=True, axis_index_groups=groups
    )


def spread(mine, axes, count):
    return exchange(jnp.broadcast_to(mine[None], (count, *mine.shape)), axes)


def dot(a, b, dims):
    return lax.dot_general(a, b, (dims, ((), ())), preferred_element_type=F32)


def gelu_exact(value):
    return 0.5 * value * (1.0 + jax.scipy.special.erf(value * 0.7071067811865476))


def gelu_slope(value):
    return (
        0.5 * (1.0 + jax.scipy.special.erf(value * 0.7071067811865476))
        + value * jnp.exp(-0.5 * value * value) * 0.3989422804014327
    )


def weight_kernel(rows_in_ref, rows_grad_ref, act_ref, pre_ref, parts_ref):
    nx, double, _ = parts_ref.shape
    block = double // 2
    in_part = dot(pre_ref[...], rows_in_ref[...], ((0,), (0,))).astype(BF)
    out_part = dot(act_ref[...], rows_grad_ref[...], ((0,), (0,))).astype(BF)
    for i in range(nx):
        parts_ref[i, :block] = in_part[i * block : (i + 1) * block]
        parts_ref[i, block:] = out_part[i * block : (i + 1) * block]


def weight_parts(rows_in, rows_grad, act, pre_grad, nx):
    count, units = act.shape
    width = rows_in.shape[1]
    block = units // nx
    tile = min(256, width)
    columns = pl.BlockSpec((count, tile), lambda i: (0, i))
    whole = pl.BlockSpec((count, units), lambda i: (0, 0))
    return pl.pallas_call(
        weight_kernel,
        grid=(width // tile,),
        in_specs=[columns, columns, whole, whole],
        out_specs=pl.BlockSpec((nx, 2 * block, tile), lambda i: (0, 0, i)),
        out_shape=jax.ShapeDtypeStruct((nx, 2 * block, width), BF),
        compiler_params=pltpu.CompilerParams(vmem_limit_bytes=VMEM_BYTES),
        cost_estimate=pl.CostEstimate(
            flops=4 * count * units * width,
            bytes_accessed=4 * rows_in.size + 4 * act.size + 4 * units * width,
            transcendentals=0,
        ),
    )(rows_in, rows_grad, act, pre_grad)


def per_device(nx, ny, nz, nl, nc, tokens, router, w_in, w_out, out_grad):
    tok, og = tokens[0], out_grad[0]
    width = tok.shape[1]
    experts = nz * nc
    block = w_out.shape[1]
    box = nx * ny * nl * nc

    at = np.arange(nx * ny * nc).reshape(nx, ny, nc)
    row_groups = [*at[:, :, 0].tolist(), *at[:, :, 1].T.tolist()]
    unit_groups = [*at[:, :, 0].T.tolist(), *at[:, :, 1].tolist()]

    weights = jnp.concatenate([w_in[0].T, w_out[0]], axis=0)
    gathered = lax.all_gather(weights, CHIPS, axis=0, tiled=False, axis_index_groups=unit_groups)

    logits = jnp.dot(tok, router, preferred_element_type=F32)
    dispatch = jax.nn.softmax(logits, axis=0)
    combine = jax.nn.softmax(logits, axis=1)
    dispatch_b = dispatch.astype(BF)
    combine_b = combine.astype(BF)
    slots = dot(dispatch_b, tok, ((0,), (0,))).astype(BF)
    slot_grad = dot(combine_b, og, ((0,), (0,))).astype(BF)
    mine = exchange(jnp.stack([slots, slot_grad], axis=1), EXPERT)
    pair = jnp.stack([mine[:, 0], mine[:, 1]], axis=0)
    rows = exchange(jnp.broadcast_to(pair[None], (ny, *pair.shape)), CHIPS, row_groups)
    rows, gathered = lax.optimization_barrier((rows, gathered))
    first = gathered[:, :block].reshape(nx * block, width)
    second = gathered[:, block:].reshape(nx * block, width)
    rows_in = rows[:, 0].reshape(ny * experts, width)
    rows_grad = rows[:, 1].reshape(ny * experts, width)

    hidden = dot(rows_in, first, ((1,), (1,)))
    act = gelu_exact(hidden).astype(BF)
    act_grad = dot(rows_grad, second, ((1,), (1,)))
    pre_grad = (act_grad * gelu_slope(hidden)).astype(BF)
    partial_out = dot(act, second, ((1,), (0,))).astype(BF)
    partial_in = dot(pre_grad, first, ((1,), (0,))).astype(BF)
    shape = (ny, experts, width)
    partial = jnp.stack([partial_out.reshape(shape), partial_in.reshape(shape)], axis=1)
    parts_of_mine = exchange(partial, CHIPS, row_groups)
    parts = weight_parts(rows_in, rows_grad, act, pre_grad, nx)
    parts_of_mine, parts = lax.optimization_barrier((parts_of_mine, parts))
    grads = lax.psum_scatter(
        parts, CHIPS, scatter_dimension=0, tiled=False, axis_index_groups=unit_groups
    )

    summed = parts_of_mine.astype(F32).sum(axis=0).astype(BF)
    back = exchange(jnp.stack([summed[0], summed[1]], axis=1), EXPERT)
    expert_out, slot_in_grad = back[:, 0], back[:, 1]

    combine_dot = dot(og, expert_out, ((1,), (1,)))
    combine_part = combine * (combine_dot - jnp.sum(combine * combine_dot, axis=1, keepdims=True))
    dispatch_dot = dot(tok, slot_in_grad, ((1,), (1,)))
    dispatch_part = dispatch * (
        dispatch_dot - jnp.sum(dispatch * dispatch_dot, axis=0, keepdims=True)
    )
    logit_grad = (combine_part + dispatch_part).astype(BF)

    local = dot(logit_grad, tok, ((0,), (0,))).astype(BF)
    pieces = exchange(local.reshape(box, 2, -1), BOX)
    piece = pieces.astype(F32).sum(axis=0).astype(BF)
    piece, grads, logit_grad = lax.optimization_barrier((piece, grads, logit_grad))
    along_z = spread(piece, "zh", nz // nl)
    w_in_grad = grads[:block].astype(F32)
    w_out_grad = grads[block:].astype(F32)
    token_grad = dot(logit_grad, router, ((1,), (1,))) + dot(
        dispatch_b, slot_in_grad, ((1,), (0,))
    )
    token_grad = token_grad.astype(BF)
    along_z, w_in_grad, w_out_grad, token_grad = lax.optimization_barrier(
        (along_z, w_in_grad, w_out_grad, token_grad)
    )
    total = along_z.astype(F32).sum(axis=0).astype(BF)
    router_grad = spread(total, BOX, box).reshape(experts, width).astype(F32).T
    return token_grad[None], router_grad, w_in_grad.T[None], w_out_grad[None]


def solution(mesh):
    dp, expert = mesh.shape["dp"], mesh.shape["expert"]
    nx, ny, nz, nl, nc = 4, dp // 4, expert // 2, 2, 2
    fine = Mesh(np.asarray(mesh.devices).reshape(nx, ny, nz // nl, nl, nc), ALL)

    def run(*args):
        return per_device(nx, ny, nz, nl, nc, *args)

    return jax.shard_map(
        run,
        mesh=fine,
        in_specs=(
            P(ALL, None, None),
            P(),
            P(EXPERT, None, ("x", "y")),
            P(EXPERT, ("x", "y"), None),
            P(ALL, None, None),
        ),
        out_specs=(
            P(ALL, None, None),
            P(),
            P(EXPERT, None, ("x", "y")),
            P(EXPERT, ("x", "y"), None),
        ),
        check_vma=False,
    )
```

```python
import jax
import jax.numpy as jnp
import numpy as np
from jax import lax
from jax.experimental import pallas as pl
from jax.experimental.pallas import tpu as pltpu
from jax.sharding import Mesh
from jax.sharding import PartitionSpec as P

BF = jnp.bfloat16
F32 = jnp.float32
Z = ("zh", "zl")
ALL = ("x", "y", "zh", "zl", "c")
EXPERT = ("zh", "zl", "c")
BOX = ("x", "y", "zl", "c")
CHIPS = ("x", "y", "c")
VMEM_BYTES = 16 * 1024 * 1024


def exchange(parts, axes, groups=None):
    return lax.all_to_all(
        parts, axes, split_axis=0, concat_axis=0, tiled=True, axis_index_groups=groups
    )


def spread(mine, axes, count):
    return exchange(jnp.broadcast_to(mine[None], (count, *mine.shape)), axes)


def dot(a, b, dims):
    return lax.dot_general(a, b, (dims, ((), ())), preferred_element_type=F32)


def gelu_exact(value):
    return 0.5 * value * (1.0 + jax.scipy.special.erf(value * 0.7071067811865476))


def gelu_slope(value):
    return (
        0.5 * (1.0 + jax.scipy.special.erf(value * 0.7071067811865476))
        + value * jnp.exp(-0.5 * value * value) * 0.3989422804014327
    )


def join_kernel(first_ref, second_ref, joint_ref):
    joint_ref[0] = first_ref[...]
    joint_ref[1] = second_ref[...]


def join(first, second):
    block, width = first.shape
    tile = block // 2
    rows = pl.BlockSpec((tile, width), lambda i: (i, 0))
    joint = pl.pallas_call(
        join_kernel,
        grid=(2,),
        in_specs=[rows, rows],
        out_specs=pl.BlockSpec((2, tile, width), lambda i: (0, i, 0)),
        out_shape=jax.ShapeDtypeStruct((2, block, width), first.dtype),
        compiler_params=pltpu.CompilerParams(vmem_limit_bytes=60 * 1024 * 1024),
        cost_estimate=pl.CostEstimate(
            flops=0, bytes_accessed=8 * first.size, transcendentals=0
        ),
    )(first, second)
    return joint.reshape(2 * block, width)


def weight_kernel(rows_in_ref, rows_grad_ref, act_ref, pre_ref, parts_ref):
    nx, double, _ = parts_ref.shape
    block = double // 2
    in_part = dot(pre_ref[...], rows_in_ref[...], ((0,), (0,))).astype(BF)
    out_part = dot(act_ref[...], rows_grad_ref[...], ((0,), (0,))).astype(BF)
    for i in range(nx):
        parts_ref[i, :block] = in_part[i * block : (i + 1) * block]
        parts_ref[i, block:] = out_part[i * block : (i + 1) * block]


def weight_parts(rows_in, rows_grad, act, pre_grad, nx):
    count, units = act.shape
    width = rows_in.shape[1]
    block = units // nx
    tile = min(256, width)
    columns = pl.BlockSpec((count, tile), lambda i: (0, i))
    whole = pl.BlockSpec((count, units), lambda i: (0, 0))
    return pl.pallas_call(
        weight_kernel,
        grid=(width // tile,),
        in_specs=[columns, columns, whole, whole],
        out_specs=pl.BlockSpec((nx, 2 * block, tile), lambda i: (0, 0, i)),
        out_shape=jax.ShapeDtypeStruct((nx, 2 * block, width), BF),
        compiler_params=pltpu.CompilerParams(vmem_limit_bytes=VMEM_BYTES),
        cost_estimate=pl.CostEstimate(
            flops=4 * count * units * width,
            bytes_accessed=4 * rows_in.size + 4 * act.size + 4 * units * width,
            transcendentals=0,
        ),
    )(rows_in, rows_grad, act, pre_grad)


def per_device(nx, ny, nz, nl, nc, tokens, router, w_in, w_out, out_grad):
    tok, og = tokens[0], out_grad[0]
    width = tok.shape[1]
    experts = nz * nc
    block = w_out.shape[1]
    box = nx * ny * nl * nc

    at = np.arange(nx * ny * nc).reshape(nx, ny, nc)
    row_groups = [*at[:, :, 0].tolist(), *at[:, :, 1].T.tolist()]
    unit_groups = [*at[:, :, 0].T.tolist(), *at[:, :, 1].tolist()]

    weights = join(w_in[0].T, w_out[0])
    gathered = lax.all_gather(weights, CHIPS, axis=0, tiled=False, axis_index_groups=unit_groups)

    logits = jnp.dot(tok, router, preferred_element_type=F32)
    dispatch = jax.nn.softmax(logits, axis=0)
    combine = jax.nn.softmax(logits, axis=1)
    dispatch_b = dispatch.astype(BF)
    combine_b = combine.astype(BF)
    slots = dot(dispatch_b, tok, ((0,), (0,))).astype(BF)
    slot_grad = dot(combine_b, og, ((0,), (0,))).astype(BF)
    mine = exchange(jnp.stack([slots, slot_grad], axis=1), EXPERT)
    pair = jnp.stack([mine[:, 0], mine[:, 1]], axis=0)
    rows = exchange(jnp.broadcast_to(pair[None], (ny, *pair.shape)), CHIPS, row_groups)
    rows, gathered = lax.optimization_barrier((rows, gathered))
    first = gathered[:, :block].reshape(nx * block, width)
    second = gathered[:, block:].reshape(nx * block, width)
    rows_in = rows[:, 0].reshape(ny * experts, width)
    rows_grad = rows[:, 1].reshape(ny * experts, width)

    hidden = dot(rows_in, first, ((1,), (1,)))
    act = gelu_exact(hidden).astype(BF)
    act_grad = dot(rows_grad, second, ((1,), (1,)))
    pre_grad = (act_grad * gelu_slope(hidden)).astype(BF)
    partial_out = dot(act, second, ((1,), (0,))).astype(BF)
    partial_in = dot(pre_grad, first, ((1,), (0,))).astype(BF)
    shape = (ny, experts, width)
    partial = jnp.stack([partial_out.reshape(shape), partial_in.reshape(shape)], axis=1)
    parts_of_mine = exchange(partial, CHIPS, row_groups)
    parts = weight_parts(rows_in, rows_grad, act, pre_grad, nx)
    parts_of_mine, parts = lax.optimization_barrier((parts_of_mine, parts))
    grads = lax.psum_scatter(
        parts, CHIPS, scatter_dimension=0, tiled=False, axis_index_groups=unit_groups
    )

    summed = parts_of_mine.astype(F32).sum(axis=0).astype(BF)
    back = exchange(jnp.stack([summed[0], summed[1]], axis=1), EXPERT)
    expert_out, slot_in_grad = back[:, 0], back[:, 1]

    combine_dot = dot(og, expert_out, ((1,), (1,)))
    combine_part = combine * (combine_dot - jnp.sum(combine * combine_dot, axis=1, keepdims=True))
    dispatch_dot = dot(tok, slot_in_grad, ((1,), (1,)))
    dispatch_part = dispatch * (
        dispatch_dot - jnp.sum(dispatch * dispatch_dot, axis=0, keepdims=True)
    )
    logit_grad = (combine_part + dispatch_part).astype(BF)

    local = dot(logit_grad, tok, ((0,), (0,))).astype(BF)
    pieces = exchange(local.reshape(box, 2, -1), BOX)
    piece = pieces.astype(F32).sum(axis=0).astype(BF)
    piece, grads, logit_grad = lax.optimization_barrier((piece, grads, logit_grad))
    along_z = spread(piece, "zh", nz // nl)
    w_in_grad = grads[:block].astype(F32)
    w_out_grad = grads[block:].astype(F32)
    token_grad = dot(logit_grad, router, ((1,), (1,))) + dot(
        dispatch_b, slot_in_grad, ((1,), (0,))
    )
    token_grad = token_grad.astype(BF)
    along_z, w_in_grad, w_out_grad, token_grad = lax.optimization_barrier(
        (along_z, w_in_grad, w_out_grad, token_grad)
    )
    total = along_z.astype(F32).sum(axis=0).astype(BF)
    router_grad = spread(total, BOX, box).reshape(experts, width).astype(F32).T
    return token_grad[None], router_grad, w_in_grad.T[None], w_out_grad[None]


def solution(mesh):
    dp, expert = mesh.shape["dp"], mesh.shape["expert"]
    nx, ny, nz, nl, nc = 4, dp // 4, expert // 2, 2, 2
    fine = Mesh(np.asarray(mesh.devices).reshape(nx, ny, nz // nl, nl, nc), ALL)

    def run(*args):
        return per_device(nx, ny, nz, nl, nc, *args)

    return jax.shard_map(
        run,
        mesh=fine,
        in_specs=(
            P(ALL, None, None),
            P(),
            P(EXPERT, None, ("x", "y")),
            P(EXPERT, ("x", "y"), None),
            P(ALL, None, None),
        ),
        out_specs=(
            P(ALL, None, None),
            P(),
            P(EXPERT, None, ("x", "y")),
            P(EXPERT, ("x", "y"), None),
        ),
        check_vma=False,
    )
```
